512 devices in a mesh: term: 8 (over y), sector: 64 (over x, z, core).
Axes of the slice: x: 4, y: 8, z: 8, core: 2. Of those that a mesh axis runs over, the one named last changes fastest.
Arguments:
- psi: float32 [4096, 32, 128], P('sector'), may hold values from -6 to 6
- left_env: float32 [4096, 24, 32, 32], P('sector', 'term'), may hold values from -1 to 1
- right_env: float32 [24, 128, 128], P('term'), may hold values from -0.5 to 0.5
- dest: int32 [4096, 8], P('sector', 'term'), may hold values from 0 to 4095, as said below
- block_rows: int32 [4096], P('sector'), may hold values from 1 to 32
Outputs:
- sigma: float32 [4096, 32, 128], P('sector', 'term')
The draws below stay inside these ranges and needn't reach their ends.
Inputs may be any that keep to these rules, and one draw needn't show every extreme that they name: Block p belongs to index p // 64 of sector. Of the 64 * 8 // 8 pairs (q, g) that one device holds, at most 2 have dest on the blocks of one index of sector, and for every device exactly 2 do for some index.
All inputs are finite; a program needn't handle non-finite values.
Results may differ from the reference program's by a relative error of at most 0.0003.
Values sent between devices are 32-bit elements; how exact they have to be, the bound alone decides.
No kernel may reach another device: no remote copies, remote signals or barrier semaphores. Data moves between devices by JAX's collectives and lax.ppermute only.
A program may use at most 64 MiB of HBM per device.

```python
import jax
import jax.numpy as jnp
from jax import lax

RB = 32
CB = 128
CH = 24
SHARE = 3
GROUPS = 8
NB_DEV = 64
NB = 4096
CAP = 2
N_TERM = 8
N_SECTOR = 64


def draw_dest(key, part):
    key = jax.random.fold_in(key, 7)
    per_dev = GROUPS // N_TERM
    count = NB_DEV * per_dev

    def single(sub):
        first, second, third, fourth = jax.random.split(sub, 4)
        heavy = jax.random.randint(first, (), 0, N_SECTOR)
        others = jax.random.permutation(second, (N_SECTOR - 1) * CAP)[:count - CAP]
        owners = jnp.concatenate([jnp.full((CAP,), heavy, jnp.int32), ((heavy + 1 + others // CAP) % N_SECTOR).astype(jnp.int32)])
        owners = jax.random.permutation(third, owners)
        places = jax.random.randint(fourth, (count,), 0, NB_DEV)
        return (owners * NB_DEV + places).astype(jnp.int32)
    values = jax.vmap(single)(jax.random.split(key, N_SECTOR * N_TERM))
    values = values.reshape(N_SECTOR, N_TERM, NB_DEV, per_dev).transpose(0, 2, 1, 3)
    return values.reshape(NB, GROUPS)


def with_ends(entries, rng, least, largest):
    longest = entries.shape.index(max(entries.shape))
    spots = []
    for shift in (0, 1):
        where = [jax.random.randint(jax.random.fold_in(rng, axis), (), 0, length) for axis, length in enumerate(entries.shape)]
        where[longest] = (where[longest] + shift) % entries.shape[longest]
        spots.append(tuple(where))
    return entries.at[spots[0]].set(least).at[spots[1]].set(largest)


def level_of(stream_key, shape, cuts, smallest, top_value):
    loudness = 1.0
    for dim, blocks in cuts:
        steps = jax.random.uniform(jax.random.fold_in(jax.random.fold_in(stream_key, 6), dim), (blocks,), jnp.float32, smallest / len(cuts), top_value / len(cuts))
        loudness = loudness * jnp.repeat(jnp.exp(steps), shape[dim] // blocks).reshape((-1,) + (1,) * (len(shape) - 1 - dim))
    return loudness


def scatter_about(own_key, extent, deviation, reach, pieces=(), kind=jnp.bfloat16):
    values = jax.random.normal(own_key, extent, jnp.float32) * deviation
    if len(pieces) > 0:
        values = level_of(own_key, extent, pieces, -0.22, 0.18) * values
    return jnp.clip(values, min=-reach, max=reach).astype(kind)


def setup_inputs(seed: int = 0) -> dict:
    key_of = jax.random.split(jax.random.key(seed), 6)
    psi = scatter_about(key_of[0], (NB, RB, CB), 1.0, 6.0, ((0, 64),), jnp.float32)
    left_env = scatter_about(key_of[1], (NB, CH, RB, RB), RB ** -0.5, 1.0, ((0, 64), (1, 8)), jnp.float32)
    right_env = scatter_about(key_of[2], (CH, CB, CB), CB ** -0.5, 0.5, ((0, 8),), jnp.float32)
    dest = draw_dest(jax.random.fold_in(key_of[5], 71), 0)
    block_rows = with_ends(jax.random.randint(key_of[4], (NB,), 1, RB + 1), jax.random.fold_in(key_of[4], 1), 1, RB).astype(jnp.int32)
    return dict(psi=psi, left_env=left_env, right_env=right_env, dest=dest, block_rows=block_rows)


def reference(psi, left_env, right_env, dest, block_rows):
    def step(total, channel):
        lefts = lax.dynamic_index_in_dim(left_env, channel, 1, keepdims=False)
        rights = lax.dynamic_index_in_dim(right_env, channel, 0, keepdims=False)
        target = lax.dynamic_index_in_dim(dest, (channel // SHARE).astype(jnp.int32), 1, keepdims=False)
        inner = jnp.einsum("qrs,qsc->qrc", lefts, psi, precision=lax.Precision.HIGHEST)
        outer = jnp.einsum("qrc,cd->qrd", inner, rights, precision=lax.Precision.HIGHEST)
        return total + jax.ops.segment_sum(outer, target, num_segments=NB), None

    start = jnp.zeros((NB, RB, CB), jnp.float32)
    total, unused = lax.scan(step, start, jnp.arange(CH, dtype=jnp.int32))
    live = jnp.arange(RB, dtype=jnp.int32)[None, :] < block_rows[:, None]
    return jnp.where(live[:, :, None], total, jnp.float32(0.0))
```

```python
import functools

import jax
import jax.numpy as jnp
from jax import lax
from jax.experimental import pallas as pl
from jax.experimental.pallas import tpu as pltpu
from jax.sharding import PartitionSpec as P

BF16, F32 = jnp.bfloat16, jnp.float32


def halves(x):
    high = x.astype(BF16)
    return high, (x - high.astype(F32)).astype(BF16)


def product_kernel(
    sectors, step, dest_ref, psi_ref, left_ref, right_ref, outbox_ref, marks_ref, rights, counts, inner
):
    blocks = dest_ref.shape[0]
    share, cols = right_ref.shape[0], right_ref.shape[1]
    rows = psi_ref.shape[1]
    pieces = outbox_ref.shape[0] // sectors
    depth = share * cols
    index = pl.program_id(0)

    @pl.when(index == 0)
    def begin():
        for k in range(share):
            high, low = halves(right_ref[k])
            rights[pl.ds(k * cols, cols), :cols] = high
            rights[pl.ds(k * cols, cols), cols:] = low
        outbox_ref[...] = jnp.zeros_like(outbox_ref)
        marks_ref[...] = jnp.zeros_like(marks_ref)

        def clear(owner, carry):
            counts[owner] = 0
            return carry

        lax.fori_loop(0, sectors, clear, 0)

    for b in range(step):
        left_high, left_low = halves(left_ref[b].reshape(share * rows, rows))
        psi_high, psi_low = halves(psi_ref[b])
        lefts = jnp.concatenate([left_high, left_low, left_high], axis=1)
        psis = jnp.concatenate([psi_high, psi_high, psi_low], axis=0)
        value = jnp.dot(lefts, psis, preferred_element_type=F32)
        for k in range(share):
            inner[pl.ds(b * rows, rows), k * cols : (k + 1) * cols] = value[k * rows : (k + 1) * rows]
    high, low = halves(inner[...])
    both = jnp.dot(high, rights[...], preferred_element_type=F32)
    items = both[:, :cols] + both[:, cols:]
    items = items + jnp.dot(low, rights[:, :cols], preferred_element_type=F32)

    place = lax.broadcasted_iota(jnp.int32, (8, cols), 0)
    lane = lax.broadcasted_iota(jnp.int32, (1, cols), 1)
    for b in range(step):
        target = dest_ref[index * step + b]
        owner, local = target // blocks, target % blocks
        slot = counts[owner]
        counts[owner] = slot + 1
        mine = (place // 4) == slot
        for v in range(rows // 8):
            whole = items[b * rows + v * 8 : b * rows + v * 8 + 8]
            turned = pltpu.roll(whole, 4, 0)
            even = jnp.where(slot == 0, whole, turned)
            odd = jnp.where(slot == 0, turned, whole)
            at = 2 * v * sectors + owner
            outbox_ref[at] = jnp.where(mine, even, outbox_ref[at])
            at = at + sectors
            outbox_ref[at] = jnp.where(mine, odd, outbox_ref[at])
        mark = (lane == slot * blocks + local).astype(F32)
        for piece in range(pieces):
            at = piece * sectors + owner
            marks_ref[at] = marks_ref[at] + mark


def products(dest, psi, left_env, right_env, sectors, terms):
    blocks, rows, cols = psi.shape
    share = right_env.shape[0]
    step = 16
    peers = sectors * terms
    return pl.pallas_call(
        functools.partial(product_kernel, sectors, step),
        grid=(blocks // step,),
        in_specs=[
            pl.BlockSpec(memory_space=pltpu.SMEM),
            pl.BlockSpec((step, rows, cols), lambda i: (i, 0, 0)),
            pl.BlockSpec((step, share, rows, rows), lambda i: (i, 0, 0, 0)),
            pl.BlockSpec((share, cols, cols), lambda i: (0, 0, 0)),
        ],
        out_specs=[
            pl.BlockSpec((peers, 8, cols), lambda i: (0, 0, 0)),
            pl.BlockSpec((peers, 1, cols), lambda i: (0, 0, 0)),
        ],
        out_shape=[
            jax.ShapeDtypeStruct((peers, 8, cols), F32),
            jax.ShapeDtypeStruct((peers, 1, cols), F32),
        ],
        scratch_shapes=[
            pltpu.VMEM((share * cols, 2 * cols), BF16),
            pltpu.SMEM((sectors,), jnp.int32),
            pltpu.VMEM((step * rows, share * cols), F32),
        ],
        compiler_params=pltpu.CompilerParams(vmem_limit_bytes=40 * 1024 * 1024),
    )(dest, psi, left_env, right_env)


def combine_kernel(term_ref, inbox_ref, marks_ref, live_ref, out_ref, total):
    index = pl.program_id(0)
    sources, rows2, cols = inbox_ref.shape
    blocks, rows = out_ref.shape[0], out_ref.shape[1]

    @pl.when(index == 0)
    def begin():
        total[...] = jnp.zeros_like(total)

    marks = marks_ref[...].reshape(sources, cols).astype(BF16)
    for slot in range(rows2 // rows):
        got = jnp.concatenate([inbox_ref[:, slot * rows + r, :] for r in range(rows)], axis=1)
        high, low = halves(got)
        select = marks[:, slot * blocks : (slot + 1) * blocks]
        dims = (((0,), (0,)), ((), ()))
        total[...] += lax.dot_general(select, high, dims, preferred_element_type=F32)
        total[...] += lax.dot_general(select, low, dims, preferred_element_type=F32)

    @pl.when(index == pl.num_programs(0) - 1)
    def end():
        for r in range(rows):
            alive = term_ref[0] * rows + r < live_ref[...]
            out_ref[:, r, :] = jnp.where(alive, total[:, r * cols : (r + 1) * cols], 0.0)


def combine(term, inbox, marks, block_rows, rows):
    peers, rows2, cols = inbox.shape
    blocks = block_rows.shape[0]
    step = 128
    return pl.pallas_call(
        combine_kernel,
        grid=(peers // step,),
        in_specs=[
            pl.BlockSpec(memory_space=pltpu.SMEM),
            pl.BlockSpec((step, rows2, cols), lambda i: (i, 0, 0)),
            pl.BlockSpec((step, 1, cols), lambda i: (i, 0, 0)),
            pl.BlockSpec((blocks, 1), lambda i: (0, 0)),
        ],
        out_specs=pl.BlockSpec((blocks, rows, cols), lambda i: (0, 0, 0)),
        out_shape=jax.ShapeDtypeStruct((blocks, rows, cols), F32),
        scratch_shapes=[pltpu.VMEM((blocks, rows * cols), F32)],
        compiler_params=pltpu.CompilerParams(vmem_limit_bytes=40 * 1024 * 1024),
    )(term, inbox, marks, block_rows.reshape(blocks, 1))


def per_device(psi, left_env, right_env, dest, block_rows):
    sectors, terms = lax.axis_size("sector"), lax.axis_size("term")
    rows = psi.shape[1] // terms
    outbox, marks = products(dest.reshape(-1), psi, left_env, right_env, sectors, terms)
    everyone = ("term", "sector")
    inbox = lax.all_to_all(outbox, everyone, split_axis=0, concat_axis=0, tiled=True)
    got_marks = lax.all_to_all(marks, everyone, split_axis=0, concat_axis=0, tiled=True)
    term = lax.axis_index("term").reshape(1)
    return combine(term, inbox, got_marks, block_rows, rows)


def solution(mesh):
    in_specs = (
        P("sector", None, None),
        P("sector", "term", None, None),
        P("term", None, None),
        P("sector", "term"),
        P("sector"),
    )
    out_specs = P("sector", "term", None)
    return jax.shard_map(
        per_device, mesh=mesh, in_specs=in_specs, out_specs=out_specs, check_vma=False
    )
```

```python
import functools

import jax
import jax.numpy as jnp
from jax import lax
from jax.experimental import pallas as pl
from jax.experimental.pallas import tpu as pltpu
from jax.sharding import PartitionSpec as P

BF16, F32 = jnp.bfloat16, jnp.float32


def halves(x):
    high = x.astype(BF16)
    return high, (x - high.astype(F32)).astype(BF16)


def product_kernel(
    sectors, step, dest_ref, psi_ref, left_ref, right_ref, outbox_ref, rights, counts, inner
):
    blocks = dest_ref.shape[0]
    share, cols = right_ref.shape[0], right_ref.shape[1]
    rows = psi_ref.shape[1]
    pieces = outbox_ref.shape[0] // sectors
    held = rows // pieces
    index = pl.program_id(0)

    @pl.when(index == 0)
    def begin():
        for k in range(share):
            high, low = halves(right_ref[k])
            rights[pl.ds(k * cols, cols), :cols] = high
            rights[pl.ds(k * cols, cols), cols:] = low
        outbox_ref[...] = jnp.zeros_like(outbox_ref)

        def clear(owner, carry):
            counts[owner] = 0
            return carry

        lax.fori_loop(0, sectors, clear, 0)

    for b in range(step):
        left_high, left_low = halves(left_ref[b].reshape(share * rows, rows))
        psi_high, psi_low = halves(psi_ref[b])
        lefts = jnp.concatenate([left_high, left_low, left_high], axis=1)
        psis = jnp.concatenate([psi_high, psi_high, psi_low], axis=0)
        value = jnp.dot(lefts, psis, preferred_element_type=F32)
        for k in range(share):
            inner[pl.ds(b * rows, rows), k * cols : (k + 1) * cols] = value[k * rows : (k + 1) * rows]
    high, low = halves(inner[...])
    both = jnp.dot(high, rights[...], preferred_element_type=F32)
    items = both[:, :cols] + both[:, cols:]
    items = items + jnp.dot(low, rights[:, :cols], preferred_element_type=F32)

    lane = lax.broadcasted_iota(jnp.int32, (1, cols), 1)
    for b in range(step):
        target = dest_ref[index * step + b]
        owner, local = target // blocks, target % blocks
        slot = counts[owner]
        counts[owner] = slot + 1
        mark = (lane == slot * blocks + local).astype(F32)
        for piece in range(pieces):
            at = piece * sectors + owner
            for r in range(held):
                row = b * rows + piece * held + r
                outbox_ref[at, slot * held + r] = items[row : row + 1]
            outbox_ref[at, 2 * held] = outbox_ref[at, 2 * held] + mark


def products(dest, psi, left_env, right_env, sectors, terms):
    blocks, rows, cols = psi.shape
    share = right_env.shape[0]
    step = 16
    peers = sectors * terms
    message = 2 * (rows // terms) + 1
    return pl.pallas_call(
        functools.partial(product_kernel, sectors, step),
        grid=(blocks // step,),
        in_specs=[
            pl.BlockSpec(memory_space=pltpu.SMEM),
            pl.BlockSpec((step, rows, cols), lambda i: (i, 0, 0)),
            pl.BlockSpec((step, share, rows, rows), lambda i: (i, 0, 0, 0)),
            pl.BlockSpec((share, cols, cols), lambda i: (0, 0, 0)),
        ],
        out_specs=pl.BlockSpec((peers, message, 1, cols), lambda i: (0, 0, 0, 0)),
        out_shape=jax.ShapeDtypeStruct((peers, message, 1, cols), F32),
        scratch_shapes=[
            pltpu.VMEM((share * cols, 2 * cols), BF16),
            pltpu.SMEM((sectors,), jnp.int32),
            pltpu.VMEM((step * rows, share * cols), F32),
        ],
        compiler_params=pltpu.CompilerParams(vmem_limit_bytes=40 * 1024 * 1024),
    )(dest, psi, left_env, right_env)


def combine_kernel(term_ref, inbox_ref, live_ref, out_ref, total):
    index = pl.program_id(0)
    cols = inbox_ref.shape[-1]
    blocks, rows = out_ref.shape[0], out_ref.shape[1]

    @pl.when(index == 0)
    def begin():
        total[...] = jnp.zeros_like(total)

    marks = inbox_ref[:, 2 * rows, 0, :].astype(BF16)
    for slot in range(2):
        got = jnp.concatenate([inbox_ref[:, slot * rows + r, 0, :] for r in range(rows)], axis=1)
        high, low = halves(got)
        select = marks[:, slot * blocks : (slot + 1) * blocks]
        dims = (((0,), (0,)), ((), ()))
        total[...] += lax.dot_general(select, high, dims, preferred_element_type=F32)
        total[...] += lax.dot_general(select, low, dims, preferred_element_type=F32)

    @pl.when(index == pl.num_programs(0) - 1)
    def end():
        for r in range(rows):
            alive = term_ref[0] * rows + r < live_ref[...]
            out_ref[:, r, :] = jnp.where(alive, total[:, r * cols : (r + 1) * cols], 0.0)


def combine(term, inbox, block_rows, rows):
    peers, message, _, cols = inbox.shape
    blocks = block_rows.shape[0]
    step = 128
    return pl.pallas_call(
        combine_kernel,
        grid=(peers // step,),
        in_specs=[
            pl.BlockSpec(memory_space=pltpu.SMEM),
            pl.BlockSpec((step, message, 1, cols), lambda i: (i, 0, 0, 0)),
            pl.BlockSpec((blocks, 1), lambda i: (0, 0)),
        ],
        out_specs=pl.BlockSpec((blocks, rows, cols), lambda i: (0, 0, 0)),
        out_shape=jax.ShapeDtypeStruct((blocks, rows, cols), F32),
        scratch_shapes=[pltpu.VMEM((blocks, rows * cols), F32)],
        compiler_params=pltpu.CompilerParams(vmem_limit_bytes=40 * 1024 * 1024),
    )(term, inbox, block_rows.reshape(blocks, 1))


def per_device(psi, left_env, right_env, dest, block_rows):
    sectors, terms = lax.axis_size("sector"), lax.axis_size("term")
    rows = psi.shape[1] // terms
    outbox = products(dest.reshape(-1), psi, left_env, right_env, sectors, terms)
    everyone = ("term", "sector")
    inbox = lax.all_to_all(outbox, everyone, split_axis=0, concat_axis=0, tiled=True)
    term = lax.axis_index("term").reshape(1)
    return combine(term, inbox, block_rows, rows)


def solution(mesh):
    in_specs = (
        P("sector", None, None),
        P("sector", "term", None, None),
        P("term", None, None),
        P("sector", "term"),
        P("sector"),
    )
    out_specs = P("sector", "term", None)
    return jax.shard_map(
        per_device, mesh=mesh, in_specs=in_specs, out_specs=out_specs, check_vma=False
    )
```

```python
import functools

import jax
import jax.numpy as jnp
from jax import lax
from jax.experimental import pallas as pl
from jax.experimental.pallas import tpu as pltpu
from jax.sharding import PartitionSpec as P

BF16, F32 = jnp.bfloat16, jnp.float32


def halves(x):
    high = x.astype(BF16)
    return high, (x - high.astype(F32)).astype(BF16)


def product_kernel(
    sectors, terms, step,
    dest_ref, psi_hbm, left_hbm, right_hbm, out_hbm,
    psi, left, right, turned, rights, counts, inner, outbox, marks, sems,
):
    blocks, rows, cols = psi.shape
    share = right.shape[0]
    held = rows // terms
    message = 2 * held + 1
    pack = cols // rows
    groups = share * rows // pack

    fetches = [
        pltpu.make_async_copy(left_hbm, left, sems.at[0]),
        pltpu.make_async_copy(right_hbm, right, sems.at[1]),
        pltpu.make_async_copy(psi_hbm, psi, sems.at[2]),
    ]
    for fetch in fetches:
        fetch.start()

    outbox[...] = jnp.zeros_like(outbox)
    marks[...] = jnp.zeros_like(marks)

    def clear(owner, carry):
        counts[owner] = 0
        return carry

    lax.fori_loop(0, sectors, clear, 0)

    fetches[0].wait()
    for g in range(groups):
        slabs = []
        for j in range(pack):
            at = j * groups + g
            slabs.append(left[at // rows, at % rows])
        slab = jnp.concatenate(slabs, axis=0)
        turned[g * blocks : (g + 1) * blocks, :] = slab.T
    fetches[1].wait()
    for k in range(share):
        high, low = halves(right[k])
        rights[k * cols : (k + 1) * cols, :cols] = high
        rights[k * cols : (k + 1) * cols, cols:] = low
    fetches[2].wait()

    lane = lax.broadcasted_iota(jnp.int32, (1, cols), 1)
    wide = lax.broadcasted_iota(jnp.int32, (groups, cols), 1)
    front, even = wide < cols // 2, (wide // rows) % 2 == 0

    def chunk(index, carry):
        for b in range(step):
            q = index * step + b
            mine = turned[pl.ds(q, groups, stride=blocks), :]
            high = mine.astype(BF16).astype(F32)
            low = mine - high
            highs = [high] + [pltpu.roll(high, rows * m, 1) for m in range(1, pack)]
            lows = [low] + [pltpu.roll(low, rows * m, 1) for m in range(1, pack)]
            parts = []
            for j in range(pack):
                h = jnp.where(front, highs[-j % pack], highs[(2 - j) % pack])
                l = jnp.where(front, lows[(1 - j) % pack], lows[(3 - j) % pack])
                parts.append(jnp.where(even, h, l))
            lefts = jnp.concatenate(parts, axis=0).astype(BF16)
            psi_high, psi_low = halves(psi[q])
            psis = jnp.concatenate([psi_high, psi_high, psi_low, psi_low], axis=0)
            value = jnp.dot(lefts, psis, preferred_element_type=F32)
            for k in range(share):
                inner[b * rows : (b + 1) * rows, k * cols : (k + 1) * cols] = value[k * rows : (k + 1) * rows]
        high, low = halves(inner[...])
        both = jnp.dot(high, rights[...], preferred_element_type=F32)
        items = both[:, :cols] + both[:, cols:]
        items = items + jnp.dot(low, rights[:, :cols], preferred_element_type=F32)
        for b in range(step):
            target = dest_ref[index * step + b]
            owner, local = target // blocks, target % blocks
            slot = counts[owner]
            counts[owner] = slot + 1
            marks[pl.ds(owner, 1), :] += (lane == slot * blocks + local).astype(F32)
            base = owner * message + slot * held
            for piece in range(terms):
                row = b * rows + piece * held
                outbox[pl.ds(base + piece * sectors * message, held), :] = items[row : row + held]
        return carry

    lax.fori_loop(0, blocks // step, chunk, 0)
    for piece in range(terms):
        at = piece * sectors * message + 2 * held
        outbox[pl.ds(at, sectors, stride=message), :] = marks[...]
    push = pltpu.make_async_copy(outbox, out_hbm, sems.at[0])
    push.start()
    push.wait()


def products(dest, psi, left_env, right_env, sectors, terms):
    blocks, rows, cols = psi.shape
    share = right_env.shape[0]
    step = 16
    message = 2 * (rows // terms) + 1
    total = sectors * terms * message
    hbm = pl.BlockSpec(memory_space=pltpu.HBM)
    out = pl.pallas_call(
        functools.partial(product_kernel, sectors, terms, step),
        in_specs=[pl.BlockSpec(memory_space=pltpu.SMEM), hbm, hbm, hbm],
        out_specs=hbm,
        out_shape=jax.ShapeDtypeStruct((total, cols), F32),
        scratch_shapes=[
            pltpu.VMEM((blocks, rows, cols), F32),
            pltpu.VMEM((share, rows, rows, blocks), F32),
            pltpu.VMEM((share, cols, cols), F32),
            pltpu.VMEM((share * rows * rows * blocks // cols, cols), F32),
            pltpu.VMEM((share * cols, 2 * cols), BF16),
            pltpu.SMEM((sectors,), jnp.int32),
            pltpu.VMEM((step * rows, share * cols), F32),
            pltpu.VMEM((total, cols), F32),
            pltpu.VMEM((sectors, cols), F32),
            pltpu.SemaphoreType.DMA((3,)),
        ],
        compiler_params=pltpu.CompilerParams(vmem_limit_bytes=60 * 1024 * 1024),
    )(dest, psi, jnp.transpose(left_env, (1, 2, 3, 0)), right_env)
    return out.reshape(sectors * terms, message, 1, cols)


def combine_kernel(term_ref, inbox_ref, live_ref, out_ref, total):
    index = pl.program_id(0)
    cols = inbox_ref.shape[-1]
    blocks, rows = out_ref.shape[0], out_ref.shape[1]

    @pl.when(index == 0)
    def begin():
        total[...] = jnp.zeros_like(total)

    marks = inbox_ref[:, 2 * rows, 0, :].astype(BF16)
    for slot in range(2):
        got = jnp.concatenate([inbox_ref[:, slot * rows + r, 0, :] for r in range(rows)], axis=1)
        high, low = halves(got)
        select = marks[:, slot * blocks : (slot + 1) * blocks]
        dims = (((0,), (0,)), ((), ()))
        total[...] += lax.dot_general(select, high, dims, preferred_element_type=F32)
        total[...] += lax.dot_general(select, low, dims, preferred_element_type=F32)

    @pl.when(index == pl.num_programs(0) - 1)
    def end():
        for r in range(rows):
            alive = term_ref[0] * rows + r < live_ref[...]
            out_ref[:, r, :] = jnp.where(alive, total[:, r * cols : (r + 1) * cols], 0.0)


def combine(term, inbox, block_rows, rows):
    peers, message, _, cols = inbox.shape
    blocks = block_rows.shape[0]
    step = 128
    return pl.pallas_call(
        combine_kernel,
        grid=(peers // step,),
        in_specs=[
            pl.BlockSpec(memory_space=pltpu.SMEM),
            pl.BlockSpec((step, message, 1, cols), lambda i: (i, 0, 0, 0)),
            pl.BlockSpec((blocks, 1), lambda i: (0, 0)),
        ],
        out_specs=pl.BlockSpec((blocks, rows, cols), lambda i: (0, 0, 0)),
        out_shape=jax.ShapeDtypeStruct((blocks, rows, cols), F32),
        scratch_shapes=[pltpu.VMEM((blocks, rows * cols), F32)],
        compiler_params=pltpu.CompilerParams(vmem_limit_bytes=40 * 1024 * 1024),
    )(term, inbox, block_rows.reshape(blocks, 1))


def per_device(psi, left_env, right_env, dest, block_rows):
    sectors, terms = lax.axis_size("sector"), lax.axis_size("term")
    rows = psi.shape[1] // terms
    outbox = products(dest.reshape(-1), psi, left_env, right_env, sectors, terms)
    inbox = lax.all_to_all(outbox, ("term", "sector"), split_axis=0, concat_axis=0, tiled=True)
    term = lax.axis_index("term").reshape(1)
    return combine(term, inbox, block_rows, rows)


def solution(mesh):
    in_specs = (
        P("sector", None, None),
        P("sector", "term", None, None),
        P("term", None, None),
        P("sector", "term"),
        P("sector"),
    )
    out_specs = P("sector", "term", None)
    return jax.shard_map(
        per_device, mesh=mesh, in_specs=in_specs, out_specs=out_specs, check_vma=False
    )
```

```python
import functools

import jax
import jax.numpy as jnp
from jax import lax
from jax.experimental import pallas as pl
from jax.experimental.pallas import tpu as pltpu
from jax.sharding import PartitionSpec as P

BF16, F32 = jnp.bfloat16, jnp.float32


def halves(x):
    high = x.astype(BF16)
    return high, (x - high.astype(F32)).astype(BF16)


def product_kernel(
    sectors, terms, step,
    dest_ref, psi_hbm, left_hbm, right_hbm, out_hbm,
    psi, left, right, turned, rights, counts, inner, outbox, marks, sems,
):
    blocks, rows, cols = psi.shape
    share = right.shape[0]
    held = rows // terms
    message = 2 * held + 1
    pack = cols // rows
    groups = share * rows // pack

    fetches = [
        pltpu.make_async_copy(left_hbm, left, sems.at[0]),
        pltpu.make_async_copy(right_hbm, right, sems.at[1]),
        pltpu.make_async_copy(psi_hbm, psi, sems.at[2]),
    ]
    for fetch in fetches:
        fetch.start()

    outbox[...] = jnp.zeros_like(outbox)
    marks[...] = jnp.zeros_like(marks)

    def clear(owner, carry):
        counts[owner] = 0
        return carry

    lax.fori_loop(0, sectors, clear, 0)

    fetches[0].wait()
    for g in range(groups):
        slabs = []
        for j in range(pack):
            at = j * groups + g
            slabs.append(left[at // rows, at % rows])
        slab = jnp.concatenate(slabs, axis=0)
        turned[g * blocks : (g + 1) * blocks, :] = slab.T
    fetches[1].wait()
    for k in range(share):
        high, low = halves(right[k])
        rights[k * cols : (k + 1) * cols, :cols] = high
        rights[k * cols : (k + 1) * cols, cols:] = low
    fetches[2].wait()

    lane = lax.broadcasted_iota(jnp.int32, (1, cols), 1)
    wide = lax.broadcasted_iota(jnp.int32, (groups, cols), 1)
    front, even = wide < cols // 2, (wide // rows) % 2 == 0

    def chunk(index, carry):
        for b in range(step):
            q = index * step + b
            mine = turned[pl.ds(q, groups, stride=blocks), :]
            high = mine.astype(BF16).astype(F32)
            low = mine - high
            highs = [high] + [pltpu.roll(high, rows * m, 1) for m in range(1, pack)]
            lows = [low] + [pltpu.roll(low, rows * m, 1) for m in range(1, pack)]
            parts = []
            for j in range(pack):
                h = jnp.where(front, highs[-j % pack], highs[(2 - j) % pack])
                l = jnp.where(front, lows[(1 - j) % pack], lows[(3 - j) % pack])
                parts.append(jnp.where(even, h, l))
            lefts = jnp.concatenate(parts, axis=0).astype(BF16)
            psi_high, psi_low = halves(psi[q])
            psis = jnp.concatenate([psi_high, psi_high, psi_low, psi_low], axis=0)
            value = jnp.dot(lefts, psis, preferred_element_type=F32)
            for k in range(share):
                inner[b * rows : (b + 1) * rows, k * cols : (k + 1) * cols] = value[k * rows : (k + 1) * rows]
        high, low = halves(inner[...])
        both = jnp.dot(high, rights[...], preferred_element_type=F32)
        items = both[:, :cols] + both[:, cols:]
        items = items + jnp.dot(low, rights[:, :cols], preferred_element_type=F32)
        for b in range(step):
            target = dest_ref[index * step + b]
            owner, local = target // blocks, target % blocks
            slot = counts[owner]
            counts[owner] = slot + 1
            marks[pl.ds(owner, 1), :] += (lane == slot * blocks + local).astype(F32)
            base = owner * message + slot * held
            for piece in range(terms):
                row = b * rows + piece * held
                outbox[pl.ds(base + piece * sectors * message, held), :] = items[row : row + held]
        return carry

    lax.fori_loop(0, blocks // step, chunk, 0)
    for piece in range(terms):
        at = piece * sectors * message + 2 * held
        outbox[pl.ds(at, sectors, stride=message), :] = marks[...]
    push = pltpu.make_async_copy(outbox, out_hbm, sems.at[0])
    push.start()
    push.wait()


def products(dest, psi, left_env, right_env, sectors, terms):
    blocks, rows, cols = psi.shape
    share = right_env.shape[0]
    step = 16
    message = 2 * (rows // terms) + 1
    total = sectors * terms * message
    hbm = pl.BlockSpec(memory_space=pltpu.HBM)
    out = pl.pallas_call(
        functools.partial(product_kernel, sectors, terms, step),
        in_specs=[pl.BlockSpec(memory_space=pltpu.SMEM), hbm, hbm, hbm],
        out_specs=hbm,
        out_shape=jax.ShapeDtypeStruct((total, cols), F32),
        scratch_shapes=[
            pltpu.VMEM((blocks, rows, cols), F32),
            pltpu.VMEM((share, rows, rows, blocks), F32),
            pltpu.VMEM((share, cols, cols), F32),
            pltpu.VMEM((share * rows * rows * blocks // cols, cols), F32),
            pltpu.VMEM((share * cols, 2 * cols), BF16),
            pltpu.SMEM((sectors,), jnp.int32),
            pltpu.VMEM((step * rows, share * cols), F32),
            pltpu.VMEM((total, cols), F32),
            pltpu.VMEM((sectors, cols), F32),
            pltpu.SemaphoreType.DMA((3,)),
        ],
        compiler_params=pltpu.CompilerParams(vmem_limit_bytes=60 * 1024 * 1024),
    )(dest, psi, jnp.transpose(left_env, (1, 2, 3, 0)), right_env)
    return out.reshape(sectors * terms, message, 1, cols)


def combine_kernel(message, term_ref, inbox_ref, live_ref, out_ref, total):
    cols = inbox_ref.shape[-1]
    blocks, rows = out_ref.shape[0], out_ref.shape[1]
    peers = inbox_ref.shape[0] // message
    step = 128
    for index in range(peers // step):

        def row(r):
            return inbox_ref[pl.ds(index * step * message + r, step, stride=message), :]

        select = row(2 * rows).astype(BF16).T
        select = jnp.concatenate([select[:blocks], select[blocks:]], axis=1)
        for r in range(rows):
            got = jnp.concatenate([row(r), row(rows + r)], axis=0)
            high, low = halves(got)
            both = jnp.dot(select, jnp.concatenate([high, low], axis=1), preferred_element_type=F32)
            value = both[:, :cols] + both[:, cols:]
            at = slice(r * cols, (r + 1) * cols)
            total[:, at] = value if index == 0 else total[:, at] + value
    for r in range(rows):
        alive = term_ref[0] * rows + r < live_ref[...]
        out_ref[:, r, :] = jnp.where(alive, total[:, r * cols : (r + 1) * cols], 0.0)


def combine(term, inbox, block_rows, rows):
    peers, message, _, cols = inbox.shape
    blocks = block_rows.shape[0]
    vmem = pl.BlockSpec(memory_space=pltpu.VMEM)
    return pl.pallas_call(
        functools.partial(combine_kernel, message),
        in_specs=[pl.BlockSpec(memory_space=pltpu.SMEM), vmem, vmem],
        out_specs=vmem,
        out_shape=jax.ShapeDtypeStruct((blocks, rows, cols), F32),
        scratch_shapes=[pltpu.VMEM((blocks, rows * cols), F32)],
        compiler_params=pltpu.CompilerParams(vmem_limit_bytes=40 * 1024 * 1024),
    )(term, inbox.reshape(peers * message, cols), block_rows.reshape(blocks, 1))


def per_device(psi, left_env, right_env, dest, block_rows):
    sectors, terms = lax.axis_size("sector"), lax.axis_size("term")
    rows = psi.shape[1] // terms
    outbox = products(dest.reshape(-1), psi, left_env, right_env, sectors, terms)
    inbox = lax.all_to_all(outbox, ("term", "sector"), split_axis=0, concat_axis=0, tiled=True)
    term = lax.axis_index("term").reshape(1)
    return combine(term, inbox, block_rows, rows)


def solution(mesh):
    in_specs = (
        P("sector", None, None),
        P("sector", "term", None, None),
        P("term", None, None),
        P("sector", "term"),
        P("sector"),
    )
    out_specs = P("sector", "term", None)
    return jax.shard_map(
        per_device, mesh=mesh, in_specs=in_specs, out_specs=out_specs, check_vma=False
    )
```

```python
import functools

import jax
import jax.numpy as jnp
from jax import lax
from jax.experimental import pallas as pl
from jax.experimental.pallas import tpu as pltpu
from jax.sharding import PartitionSpec as P

BF16, F32 = jnp.bfloat16, jnp.float32


def halves(x):
    high = x.astype(BF16)
    return high, (x - high.astype(F32)).astype(BF16)


def product_kernel(
    sectors, terms,
    dest_ref, psi_hbm, left_hbm, right_hbm, out_hbm,
    psi, left, right, turned, rights, counts, outbox, marks, middle, sems,
):
    blocks, rows, cols = psi.shape
    share = right.shape[0]
    held = rows // terms
    message = 2 * held + 1

    fetch_right = pltpu.make_async_copy(right_hbm, right, sems.at[0])
    step, span = blocks // 2, rows // 1
    fetch_psi, fetch_left = [], []
    for i in range(2):
        part = pl.ds(i * step, step)
        fetch_psi.append(pltpu.make_async_copy(psi_hbm.at[part], psi.at[part], sems.at[1 + i]))
    for i in range(1):
        part = pl.ds(i * span, span)
        fetch_left.append(
            pltpu.make_async_copy(left_hbm.at[:, part], left.at[:, part], sems.at[1 + 2 + i])
        )
    fetch_right.start()
    for fetch in fetch_psi:
        fetch.start()
    for fetch in fetch_left:
        fetch.start()

    outbox[...] = jnp.zeros_like(outbox)
    marks[...] = jnp.zeros_like(marks)

    def clear(owner, carry):
        counts[owner] = 0
        return carry

    lax.fori_loop(0, sectors, clear, 0)

    fetch_right.wait()
    for k in range(share):
        high, low = halves(right[k])
        rights[:cols, k * cols : (k + 1) * cols] = high
        rights[cols : 2 * cols, k * cols : (k + 1) * cols] = high
        rights[2 * cols :, k * cols : (k + 1) * cols] = low

    def first(index, carry):
        value = psi[pl.ds(index * step, step)].reshape(step * rows, cols)
        high, low = halves(value)
        stacked = jnp.concatenate([high, low, high], axis=1)
        value = jnp.dot(stacked, rights[...], preferred_element_type=F32)
        high, low = halves(value)
        for b in range(step):
            for k in range(share):
                at = slice(k * rows, (k + 1) * rows)
                part = (slice(b * rows, (b + 1) * rows), slice(k * cols, (k + 1) * cols))
                middle[index * step + b, at, :cols] = high[part]
                middle[index * step + b, at, cols:] = low[part]
        return carry

    for index, fetch in enumerate(fetch_psi):
        fetch.wait()
        first(index, 0)

    for r in range(rows):
        if r % span == 0:
            fetch_left[r // span].wait()
        slab = jnp.concatenate([left[k, r] for k in range(share)], axis=0)
        turned[r * blocks : (r + 1) * blocks, :] = slab.T

    lane = lax.broadcasted_iota(jnp.int32, (1, cols), 1)

    def second(index, carry):
        for b in range(step):
            q = index * step + b
            high, low = halves(turned[pl.ds(q, rows, stride=blocks), :])
            both = jnp.dot(
                jnp.concatenate([high, low], axis=0), middle[q], preferred_element_type=F32
            )
            item = both[:rows, :cols] + (both[:rows, cols:] + both[rows:, :cols])
            target = dest_ref[q]
            owner, local = target // blocks, target % blocks
            slot = counts[owner]
            counts[owner] = slot + 1
            marks[pl.ds(owner, 1), :] += (lane == slot * blocks + local).astype(F32)
            base = owner * message + slot * held
            for piece in range(terms):
                outbox[pl.ds(base + piece * sectors * message, held), :] = item[
                    piece * held : (piece + 1) * held
                ]
        return carry

    for index in range(blocks // step):
        second(index, 0)
    for piece in range(terms):
        at = piece * sectors * message + 2 * held
        outbox[pl.ds(at, sectors, stride=message), :] = marks[...]
    push = pltpu.make_async_copy(outbox, out_hbm, sems.at[0])
    push.start()
    push.wait()


def products(dest, psi, left_env, right_env, sectors, terms):
    blocks, rows, cols = psi.shape
    share = right_env.shape[0]
    message = 2 * (rows // terms) + 1
    total = sectors * terms * message
    hbm = pl.BlockSpec(memory_space=pltpu.HBM)
    out = pl.pallas_call(
        functools.partial(product_kernel, sectors, terms),
        in_specs=[pl.BlockSpec(memory_space=pltpu.SMEM), hbm, hbm, hbm],
        out_specs=hbm,
        out_shape=jax.ShapeDtypeStruct((total, cols), F32),
        scratch_shapes=[
            pltpu.VMEM((blocks, rows, cols), F32),
            pltpu.VMEM((share, rows, rows, blocks), F32),
            pltpu.VMEM((share, cols, cols), F32),
            pltpu.VMEM((rows * blocks, share * rows), F32),
            pltpu.VMEM((3 * cols, share * cols), BF16),
            pltpu.SMEM((sectors,), jnp.int32),
            pltpu.VMEM((total, cols), F32),
            pltpu.VMEM((sectors, cols), F32),
            pltpu.VMEM((blocks, share * rows, 2 * cols), BF16),
            pltpu.SemaphoreType.DMA((4,)),
        ],
        compiler_params=pltpu.CompilerParams(vmem_limit_bytes=60 * 1024 * 1024),
    )(dest, psi, jnp.transpose(left_env, (1, 2, 3, 0)), right_env)
    return out.reshape(sectors * terms, message, 1, cols)


def combine_kernel(message, term_ref, inbox_ref, live_ref, out_ref, total):
    cols = inbox_ref.shape[-1]
    blocks, rows = out_ref.shape[0], out_ref.shape[1]
    peers = inbox_ref.shape[0] // message
    step = 128
    for index in range(peers // step):

        def row(r):
            return inbox_ref[pl.ds(index * step * message + r, step, stride=message), :]

        select = row(2 * rows).astype(BF16).T
        select = jnp.concatenate([select[:blocks], select[blocks:]], axis=1)
        for r in range(rows):
            got = jnp.concatenate([row(r), row(rows + r)], axis=0)
            high, low = halves(got)
            both = jnp.dot(select, jnp.concatenate([high, low], axis=1), preferred_element_type=F32)
            value = both[:, :cols] + both[:, cols:]
            at = slice(r * cols, (r + 1) * cols)
            total[:, at] = value if index == 0 else total[:, at] + value
    for r in range(rows):
        alive = term_ref[0] * rows + r < live_ref[...]
        out_ref[:, r, :] = jnp.where(alive, total[:, r * cols : (r + 1) * cols], 0.0)


def combine(term, inbox, block_rows, rows):
    peers, message, _, cols = inbox.shape
    blocks = block_rows.shape[0]
    vmem = pl.BlockSpec(memory_space=pltpu.VMEM)
    return pl.pallas_call(
        functools.partial(combine_kernel, message),
        in_specs=[pl.BlockSpec(memory_space=pltpu.SMEM), vmem, vmem],
        out_specs=vmem,
        out_shape=jax.ShapeDtypeStruct((blocks, rows, cols), F32),
        scratch_shapes=[pltpu.VMEM((blocks, rows * cols), F32)],
        compiler_params=pltpu.CompilerParams(vmem_limit_bytes=40 * 1024 * 1024),
    )(term, inbox.reshape(peers * message, cols), block_rows.reshape(blocks, 1))


def per_device(psi, left_env, right_env, dest, block_rows):
    sectors, terms = lax.axis_size("sector"), lax.axis_size("term")
    rows = psi.shape[1] // terms
    outbox = products(dest.reshape(-1), psi, left_env, right_env, sectors, terms)
    inbox = lax.all_to_all(outbox, ("term", "sector"), split_axis=0, concat_axis=0, tiled=True)
    term = lax.axis_index("term").reshape(1)
    return combine(term, inbox, block_rows, rows)


def solution(mesh):
    in_specs = (
        P("sector", None, None),
        P("sector", "term", None, None),
        P("term", None, None),
        P("sector", "term"),
        P("sector"),
    )
    out_specs = P("sector", "term", None)
    return jax.shard_map(
        per_device, mesh=mesh, in_specs=in_specs, out_specs=out_specs, check_vma=False
    )
```

```python
import functools

import jax
import jax.numpy as jnp
from jax import lax
from jax.experimental import pallas as pl
from jax.experimental.pallas import tpu as pltpu
from jax.sharding import PartitionSpec as P

BF16, F32 = jnp.bfloat16, jnp.float32


def halves(x):
    high = x.astype(BF16)
    return high, (x - high.astype(F32)).astype(BF16)


def product_kernel(
    sectors, terms,
    dest_ref, psi_hbm, left_hbm, right_hbm, out_hbm,
    psi, left, right, turned, rights, counts, places, outbox, marks, middle, sems,
):
    blocks, rows, cols = psi.shape
    share = right.shape[0]
    held = rows // terms
    message = 2 * held + 1

    fetch_right = pltpu.make_async_copy(right_hbm, right, sems.at[0])
    fetch_left = pltpu.make_async_copy(left_hbm, left, sems.at[1])
    fetch_psi = []
    step = blocks // 2
    for i in range(2):
        part = pl.ds(i * step, step)
        fetch_psi.append(pltpu.make_async_copy(psi_hbm.at[part], psi.at[part], sems.at[2 + i]))
    fetch_right.start()
    for fetch in fetch_psi:
        fetch.start()
    fetch_left.start()

    outbox[...] = jnp.zeros_like(outbox)
    marks[...] = jnp.zeros_like(marks)

    def clear(owner, carry):
        counts[owner] = 0
        return carry

    lax.fori_loop(0, sectors, clear, 0)

    fetch_right.wait()
    for k in range(share):
        high, low = halves(right[k])
        rights[:cols, k * cols : (k + 1) * cols] = high
        rights[cols : 2 * cols, k * cols : (k + 1) * cols] = high
        rights[2 * cols :, k * cols : (k + 1) * cols] = low

    def first(index, carry):
        value = psi[pl.ds(index * step, step)].reshape(step * rows, cols)
        high, low = halves(value)
        stacked = jnp.concatenate([high, low, high], axis=1)
        value = jnp.dot(stacked, rights[...], preferred_element_type=F32)
        high, low = halves(value)
        for b in range(step):
            for k in range(share):
                at = slice(k * rows, (k + 1) * rows)
                part = (slice(b * rows, (b + 1) * rows), slice(k * cols, (k + 1) * cols))
                middle[index * step + b, at, :cols] = high[part]
                middle[index * step + b, at, cols:] = low[part]
        return carry

    for index, fetch in enumerate(fetch_psi):
        fetch.wait()
        first(index, 0)

    fetch_left.wait()
    for r in range(rows):
        slab = jnp.concatenate([left[k, r] for k in range(share)], axis=0)
        turned[r * blocks : (r + 1) * blocks, :] = slab.T

    lane = lax.broadcasted_iota(jnp.int32, (1, cols), 1)
    for q in range(blocks):
        target = dest_ref[q]
        owner, local = target // blocks, target % blocks
        slot = counts[owner]
        counts[owner] = slot + 1
        places[q] = owner * message + slot * held
        marks[pl.ds(owner, 1), :] += (lane == slot * blocks + local).astype(F32)

    span = rows // 2
    pushes = []
    for begin in range(0, rows, span):
        for q in range(blocks):
            mine = turned[pl.ds(begin * blocks + q, span, stride=blocks), :]
            high, low = halves(mine)
            both = jnp.dot(
                jnp.concatenate([high, low], axis=0), middle[q], preferred_element_type=F32
            )
            item = both[:span, :cols] + (both[:span, cols:] + both[span:, :cols])
            for at in range(0, span, held):
                piece = (begin + at) // held
                outbox[pl.ds(places[q] + piece * sectors * message, held), :] = item[at : at + held]
        for piece in range(begin // held, (begin + span) // held):
            at = piece * sectors * message + 2 * held
            outbox[pl.ds(at, sectors, stride=message), :] = marks[:sectors, :]
        size = span // held * sectors * message
        part = pl.ds(begin // held * sectors * message, size)
        push = pltpu.make_async_copy(outbox.at[part], out_hbm.at[part], sems.at[len(pushes)])
        push.start()
        pushes.append(push)
    for push in pushes:
        push.wait()


def products(dest, psi, left_env, right_env, sectors, terms):
    blocks, rows, cols = psi.shape
    share = right_env.shape[0]
    message = 2 * (rows // terms) + 1
    total = sectors * terms * message
    hbm = pl.BlockSpec(memory_space=pltpu.HBM)
    out = pl.pallas_call(
        functools.partial(product_kernel, sectors, terms),
        in_specs=[pl.BlockSpec(memory_space=pltpu.SMEM), hbm, hbm, hbm],
        out_specs=hbm,
        out_shape=jax.ShapeDtypeStruct((total, cols), F32),
        scratch_shapes=[
            pltpu.VMEM((blocks, rows, cols), F32),
            pltpu.VMEM((share, rows, rows, blocks), F32),
            pltpu.VMEM((share, cols, cols), F32),
            pltpu.VMEM((rows * blocks + blocks, share * rows), F32),
            pltpu.VMEM((3 * cols, share * cols), BF16),
            pltpu.SMEM((sectors,), jnp.int32),
            pltpu.SMEM((blocks,), jnp.int32),
            pltpu.VMEM((total + 8, cols), F32),
            pltpu.VMEM((sectors + 8, cols), F32),
            pltpu.VMEM((blocks, share * rows, 2 * cols), BF16),
            pltpu.SemaphoreType.DMA((4,)),
        ],
        compiler_params=pltpu.CompilerParams(vmem_limit_bytes=60 * 1024 * 1024),
    )(dest, psi, jnp.transpose(left_env, (1, 2, 3, 0)), right_env)
    return out.reshape(sectors * terms, message, 1, cols)


def combine_kernel(message, term_ref, inbox_ref, live_ref, out_ref, total):
    cols = inbox_ref.shape[-1]
    blocks, rows = out_ref.shape[0], out_ref.shape[1]
    peers = inbox_ref.shape[0] // message
    step = 128
    for index in range(peers // step):

        def row(r):
            return inbox_ref[pl.ds(index * step * message + r, step, stride=message), :]

        select = row(2 * rows).astype(BF16).T
        select = jnp.concatenate([select[:blocks], select[blocks:]], axis=1)
        for r in range(rows):
            got = jnp.concatenate([row(r), row(rows + r)], axis=0)
            high, low = halves(got)
            both = jnp.dot(select, jnp.concatenate([high, low], axis=1), preferred_element_type=F32)
            value = both[:, :cols] + both[:, cols:]
            at = slice(r * cols, (r + 1) * cols)
            total[:, at] = value if index == 0 else total[:, at] + value
    for r in range(rows):
        alive = term_ref[0] * rows + r < live_ref[...]
        out_ref[:, r, :] = jnp.where(alive, total[:, r * cols : (r + 1) * cols], 0.0)


def combine(term, inbox, block_rows, rows):
    peers, message, _, cols = inbox.shape
    blocks = block_rows.shape[0]
    vmem = pl.BlockSpec(memory_space=pltpu.VMEM)
    return pl.pallas_call(
        functools.partial(combine_kernel, message),
        in_specs=[pl.BlockSpec(memory_space=pltpu.SMEM), vmem, vmem],
        out_specs=vmem,
        out_shape=jax.ShapeDtypeStruct((blocks, rows, cols), F32),
        scratch_shapes=[pltpu.VMEM((blocks, rows * cols), F32)],
        compiler_params=pltpu.CompilerParams(vmem_limit_bytes=40 * 1024 * 1024),
    )(term, inbox.reshape(peers * message, cols), block_rows.reshape(blocks, 1))


def per_device(psi, left_env, right_env, dest, block_rows):
    sectors, terms = lax.axis_size("sector"), lax.axis_size("term")
    rows = psi.shape[1] // terms
    outbox = products(dest.reshape(-1), psi, left_env, right_env, sectors, terms)
    inbox = lax.all_to_all(outbox, ("term", "sector"), split_axis=0, concat_axis=0, tiled=True)
    term = lax.axis_index("term").reshape(1)
    return combine(term, inbox, block_rows, rows)


def solution(mesh):
    in_specs = (
        P("sector", None, None),
        P("sector", "term", None, None),
        P("term", None, None),
        P("sector", "term"),
        P("sector"),
    )
    out_specs = P("sector", "term", None)
    return jax.shard_map(
        per_device, mesh=mesh, in_specs=in_specs, out_specs=out_specs, check_vma=False
    )
```

```python
import functools

import jax
import jax.numpy as jnp
from jax import lax
from jax.experimental import pallas as pl
from jax.experimental.pallas import tpu as pltpu
from jax.sharding import PartitionSpec as P

BF16, F32 = jnp.bfloat16, jnp.float32


def halves(x):
    high = x.astype(BF16)
    return high, (x - high.astype(F32)).astype(BF16)


def product_kernel(
    sectors, terms,
    dest_ref, psi_hbm, left_hbm, right_hbm, out_hbm,
    psi, left, right, turned, rights, counts, places, outbox, marks, middle, sems,
):
    blocks, rows, cols = psi.shape
    share = right.shape[0]
    held = rows // terms
    message = 2 * held + 1

    fetch_right = pltpu.make_async_copy(right_hbm, right, sems.at[0])
    fetch_left = pltpu.make_async_copy(left_hbm, left, sems.at[1])
    fetch_psi = []
    step = blocks // 2
    for i in range(2):
        part = pl.ds(i * step, step)
        fetch_psi.append(pltpu.make_async_copy(psi_hbm.at[part], psi.at[part], sems.at[2 + i]))
    fetch_right.start()
    for fetch in fetch_psi:
        fetch.start()
    fetch_left.start()

    outbox[...] = jnp.zeros_like(outbox)
    marks[...] = jnp.zeros_like(marks)

    def clear(owner, carry):
        counts[owner] = 0
        return carry

    lax.fori_loop(0, sectors, clear, 0)

    fetch_right.wait()
    for k in range(share):
        high, low = halves(right[k])
        rights[:cols, k * cols : (k + 1) * cols] = high
        rights[cols : 2 * cols, k * cols : (k + 1) * cols] = high
        rights[2 * cols :, k * cols : (k + 1) * cols] = low

    def first(index, carry):
        value = psi[pl.ds(index * step, step)].reshape(step * rows, cols)
        high, low = halves(value)
        stacked = jnp.concatenate([high, low, high], axis=1)
        value = jnp.dot(stacked, rights[...], preferred_element_type=F32)
        high, low = halves(value)
        for b in range(step):
            for k in range(share):
                at = slice(k * rows, (k + 1) * rows)
                part = (slice(b * rows, (b + 1) * rows), slice(k * cols, (k + 1) * cols))
                middle[index * step + b, at, :cols] = high[part]
                middle[index * step + b, at, cols:] = low[part]
        return carry

    for index, fetch in enumerate(fetch_psi):
        fetch.wait()
        first(index, 0)

    fetch_left.wait()
    for r in range(rows):
        slab = jnp.concatenate([left[k, r] for k in range(share)], axis=0)
        turned[r * blocks : (r + 1) * blocks, :] = slab.T

    lane = lax.broadcasted_iota(jnp.int32, (1, cols), 1)
    for q in range(blocks):
        target = dest_ref[q]
        owner, local = target // blocks, target % blocks
        slot = counts[owner]
        counts[owner] = slot + 1
        places[q] = owner * terms * message + slot * held
        marks[pl.ds(owner, 1), :] += (lane == slot * blocks + local).astype(F32)

    for q in range(blocks):
        high, low = halves(turned[pl.ds(q, rows, stride=blocks), :])
        both = jnp.dot(
            jnp.concatenate([high, low], axis=0), middle[q], preferred_element_type=F32
        )
        item = both[:rows, :cols] + (both[:rows, cols:] + both[rows:, :cols])
        for piece in range(terms):
            at = places[q] + piece * message
            outbox[pl.ds(at, held), :] = item[piece * held : (piece + 1) * held]
    for piece in range(terms):
        at = piece * message + 2 * held
        outbox[pl.ds(at, sectors, stride=terms * message), :] = marks[:sectors, :]
    total = sectors * terms * message
    push = pltpu.make_async_copy(outbox.at[pl.ds(0, total)], out_hbm, sems.at[0])
    push.start()
    push.wait()


def products(dest, psi, left_env, right_env, sectors, terms):
    blocks, rows, cols = psi.shape
    share = right_env.shape[0]
    message = 2 * (rows // terms) + 1
    total = sectors * terms * message
    hbm = pl.BlockSpec(memory_space=pltpu.HBM)
    out = pl.pallas_call(
        functools.partial(product_kernel, sectors, terms),
        in_specs=[pl.BlockSpec(memory_space=pltpu.SMEM), hbm, hbm, hbm],
        out_specs=hbm,
        out_shape=jax.ShapeDtypeStruct((total, cols), F32),
        scratch_shapes=[
            pltpu.VMEM((blocks, rows, cols), F32),
            pltpu.VMEM((share, rows, rows, blocks), F32),
            pltpu.VMEM((share, cols, cols), F32),
            pltpu.VMEM((rows * blocks + blocks, share * rows), F32),
            pltpu.VMEM((3 * cols, share * cols), BF16),
            pltpu.SMEM((sectors,), jnp.int32),
            pltpu.SMEM((blocks,), jnp.int32),
            pltpu.VMEM((total + 8, cols), F32),
            pltpu.VMEM((sectors + 8, cols), F32),
            pltpu.VMEM((blocks, share * rows, 2 * cols), BF16),
            pltpu.SemaphoreType.DMA((4,)),
        ],
        compiler_params=pltpu.CompilerParams(vmem_limit_bytes=60 * 1024 * 1024),
    )(dest, psi, jnp.transpose(left_env, (1, 2, 3, 0)), right_env)
    return out.reshape(sectors * terms, message, 1, cols)


def combine_kernel(message, term_ref, inbox_ref, live_ref, out_ref, total):
    cols = inbox_ref.shape[-1]
    blocks, rows = out_ref.shape[0], out_ref.shape[1]
    peers = inbox_ref.shape[0] // message
    step = 128
    for index in range(peers // step):

        def row(r):
            return inbox_ref[pl.ds(index * step * message + r, step, stride=message), :]

        select = row(2 * rows).astype(BF16).T
        select = jnp.concatenate([select[:blocks], select[blocks:]], axis=1)
        for r in range(rows):
            got = jnp.concatenate([row(r), row(rows + r)], axis=0)
            high, low = halves(got)
            both = jnp.dot(select, jnp.concatenate([high, low], axis=1), preferred_element_type=F32)
            value = both[:, :cols] + both[:, cols:]
            at = slice(r * cols, (r + 1) * cols)
            total[:, at] = value if index == 0 else total[:, at] + value
    for r in range(rows):
        alive = term_ref[0] * rows + r < live_ref[...]
        out_ref[:, r, :] = jnp.where(alive, total[:, r * cols : (r + 1) * cols], 0.0)


def combine(term, inbox, block_rows, rows):
    peers, message, _, cols = inbox.shape
    blocks = block_rows.shape[0]
    vmem = pl.BlockSpec(memory_space=pltpu.VMEM)
    return pl.pallas_call(
        functools.partial(combine_kernel, message),
        in_specs=[pl.BlockSpec(memory_space=pltpu.SMEM), vmem, vmem],
        out_specs=vmem,
        out_shape=jax.ShapeDtypeStruct((blocks, rows, cols), F32),
        scratch_shapes=[pltpu.VMEM((blocks, rows * cols), F32)],
        compiler_params=pltpu.CompilerParams(vmem_limit_bytes=40 * 1024 * 1024),
    )(term, inbox.reshape(peers * message, cols), block_rows.reshape(blocks, 1))


def per_device(psi, left_env, right_env, dest, block_rows):
    sectors, terms = lax.axis_size("sector"), lax.axis_size("term")
    rows = psi.shape[1] // terms
    outbox = products(dest.reshape(-1), psi, left_env, right_env, sectors, terms)
    inbox = lax.all_to_all(outbox, ("sector", "term"), split_axis=0, concat_axis=0, tiled=True)
    term = lax.axis_index("term").reshape(1)
    return combine(term, inbox, block_rows, rows)


def solution(mesh):
    in_specs = (
        P("sector", None, None),
        P("sector", "term", None, None),
        P("term", None, None),
        P("sector", "term"),
        P("sector"),
    )
    out_specs = P("sector", "term", None)
    return jax.shard_map(
        per_device, mesh=mesh, in_specs=in_specs, out_specs=out_specs, check_vma=False
    )
```

```python
import functools

import jax
import jax.numpy as jnp
from jax import lax
from jax.experimental import pallas as pl
from jax.experimental.pallas import tpu as pltpu
from jax.sharding import PartitionSpec as P

BF16, F32 = jnp.bfloat16, jnp.float32


def halves(x):
    high = x.astype(BF16)
    return high, (x - high.astype(F32)).astype(BF16)


def product_kernel(
    sectors, terms,
    dest_ref, psi_hbm, left_hbm, right_hbm, out_hbm,
    psi, left, right, turned, rights, counts, places, outbox, marks, middle, sems,
):
    blocks, rows, cols = psi.shape
    share = right.shape[0]
    held = rows // terms
    message = 2 * held + 1

    fetch_right = pltpu.make_async_copy(right_hbm, right, sems.at[0])
    fetch_left = pltpu.make_async_copy(left_hbm, left, sems.at[1])
    fetch_psi = []
    step = blocks // 2
    for i in range(2):
        part = pl.ds(i * step, step)
        fetch_psi.append(pltpu.make_async_copy(psi_hbm.at[part], psi.at[part], sems.at[2 + i]))
    fetch_right.start()
    for fetch in fetch_psi:
        fetch.start()
    fetch_left.start()

    outbox[...] = jnp.zeros_like(outbox)
    marks[...] = jnp.zeros_like(marks)

    def clear(owner, carry):
        counts[owner] = 0
        return carry

    lax.fori_loop(0, sectors, clear, 0)

    fetch_right.wait()
    for k in range(share):
        high, low = halves(right[k])
        rights[:cols, k * cols : (k + 1) * cols] = high
        rights[cols : 2 * cols, k * cols : (k + 1) * cols] = high
        rights[2 * cols :, k * cols : (k + 1) * cols] = low

    def first(index, carry):
        value = psi[pl.ds(index * step, step)].reshape(step * rows, cols)
        high, low = halves(value)
        stacked = jnp.concatenate([high, low, high], axis=1)
        value = jnp.dot(stacked, rights[...], preferred_element_type=F32)
        high, low = halves(value)
        for b in range(step):
            for k in range(share):
                at = slice(k * rows, (k + 1) * rows)
                part = (slice(b * rows, (b + 1) * rows), slice(k * cols, (k + 1) * cols))
                middle[index * step + b, at, :cols] = high[part]
                middle[index * step + b, at, cols:] = low[part]
        return carry

    for index, fetch in enumerate(fetch_psi):
        fetch.wait()
        first(index, 0)

    fetch_left.wait()
    for r in range(rows):
        slab = jnp.concatenate([left[k, r] for k in range(share)], axis=0)
        turned[r * blocks : (r + 1) * blocks, :] = slab.T

    lane = lax.broadcasted_iota(jnp.int32, (1, cols), 1)
    for q in range(blocks):
        target = dest_ref[q]
        owner, local = target // blocks, target % blocks
        slot = counts[owner]
        counts[owner] = slot + 1
        places[q] = owner * terms * message + slot * held
        marks[pl.ds(owner, 1), :] += (lane == slot * blocks + local).astype(F32)

    for q in range(blocks):
        high, low = halves(turned[pl.ds(q, rows, stride=blocks), :])
        both = jnp.dot(
            jnp.concatenate([high, low], axis=0), middle[q], preferred_element_type=F32
        )
        item = both[:rows, :cols] + (both[:rows, cols:] + both[rows:, :cols])
        for piece in range(terms):
            at = places[q] + piece * message
            outbox[pl.ds(at, held), :] = item[piece * held : (piece + 1) * held]
    for piece in range(terms):
        at = piece * message + 2 * held
        outbox[pl.ds(at, sectors, stride=terms * message), :] = marks[:sectors, :]
    total = sectors * terms * message
    push = pltpu.make_async_copy(outbox.at[pl.ds(0, total)], out_hbm, sems.at[0])
    push.start()
    push.wait()


def products(dest, psi, left_env, right_env, sectors, terms):
    blocks, rows, cols = psi.shape
    share = right_env.shape[0]
    message = 2 * (rows // terms) + 1
    total = sectors * terms * message
    hbm = pl.BlockSpec(memory_space=pltpu.HBM)
    out = pl.pallas_call(
        functools.partial(product_kernel, sectors, terms),
        in_specs=[pl.BlockSpec(memory_space=pltpu.SMEM), hbm, hbm, hbm],
        out_specs=hbm,
        out_shape=jax.ShapeDtypeStruct((total, cols), F32),
        scratch_shapes=[
            pltpu.VMEM((blocks, rows, cols), F32),
            pltpu.VMEM((share, rows, rows, blocks), F32),
            pltpu.VMEM((share, cols, cols), F32),
            pltpu.VMEM((rows * blocks + blocks, share * rows), F32),
            pltpu.VMEM((3 * cols, share * cols), BF16),
            pltpu.SMEM((sectors,), jnp.int32),
            pltpu.SMEM((blocks,), jnp.int32),
            pltpu.VMEM((total + terms * message + 8, cols), F32),
            pltpu.VMEM((sectors + 8, cols), F32),
            pltpu.VMEM((blocks, share * rows, 2 * cols), BF16),
            pltpu.SemaphoreType.DMA((4,)),
        ],
        compiler_params=pltpu.CompilerParams(vmem_limit_bytes=60 * 1024 * 1024),
    )(dest, psi, jnp.transpose(left_env, (1, 2, 3, 0)), right_env)
    return out.reshape(sectors * terms, message, 1, cols)


def combine_kernel(message, term_ref, inbox_ref, live_ref, out_ref, total):
    cols = inbox_ref.shape[-1]
    blocks, rows = out_ref.shape[0], out_ref.shape[1]
    peers = inbox_ref.shape[0] // message
    step = 128
    for index in range(peers // step):

        def row(r):
            return inbox_ref[pl.ds(index * step * message + r, step, stride=message), :]

        select = row(2 * rows).astype(BF16).T
        select = jnp.concatenate([select[:blocks], select[blocks:]], axis=1)
        for r in range(rows):
            got = jnp.concatenate([row(r), row(rows + r)], axis=0)
            high, low = halves(got)
            both = jnp.dot(select, jnp.concatenate([high, low], axis=1), preferred_element_type=F32)
            value = both[:, :cols] + both[:, cols:]
            at = slice(r * cols, (r + 1) * cols)
            total[:, at] = value if index == 0 else total[:, at] + value
    for r in range(rows):
        alive = term_ref[0] * rows + r < live_ref[...]
        out_ref[:, r, :] = jnp.where(alive, total[:, r * cols : (r + 1) * cols], 0.0)


def combine(term, inbox, block_rows, rows):
    peers, message, _, cols = inbox.shape
    blocks = block_rows.shape[0]
    vmem = pl.BlockSpec(memory_space=pltpu.VMEM)
    return pl.pallas_call(
        functools.partial(combine_kernel, message),
        in_specs=[pl.BlockSpec(memory_space=pltpu.SMEM), vmem, vmem],
        out_specs=vmem,
        out_shape=jax.ShapeDtypeStruct((blocks, rows, cols), F32),
        scratch_shapes=[pltpu.VMEM((blocks, rows * cols), F32)],
        compiler_params=pltpu.CompilerParams(vmem_limit_bytes=40 * 1024 * 1024),
    )(term, inbox.reshape(peers * message, cols), block_rows.reshape(blocks, 1))


def per_device(psi, left_env, right_env, dest, block_rows):
    sectors, terms = lax.axis_size("sector"), lax.axis_size("term")
    rows = psi.shape[1] // terms
    outbox = products(dest.reshape(-1), psi, left_env, right_env, sectors, terms)
    inbox = lax.all_to_all(outbox, ("sector", "term"), split_axis=0, concat_axis=0, tiled=True)
    term = lax.axis_index("term").reshape(1)
    return combine(term, inbox, block_rows, rows)


def solution(mesh):
    in_specs = (
        P("sector", None, None),
        P("sector", "term", None, None),
        P("term", None, None),
        P("sector", "term"),
        P("sector"),
    )
    out_specs = P("sector", "term", None)
    return jax.shard_map(
        per_device, mesh=mesh, in_specs=in_specs, out_specs=out_specs, check_vma=False
    )
```

```python
import functools

import jax
import jax.numpy as jnp
from jax import lax
from jax.experimental import pallas as pl
from jax.experimental.pallas import tpu as pltpu
from jax.sharding import PartitionSpec as P

BF16, F32 = jnp.bfloat16, jnp.float32


def halves(x):
    high = x.astype(BF16)
    return high, (x - high.astype(F32)).astype(BF16)


def product_kernel(
    sectors, terms,
    dest_ref, psi_hbm, left_hbm, right_hbm, out_hbm,
    psi, left, right, turned, rights, counts, places, outbox, marks, middle, sems,
):
    blocks, rows, cols = psi.shape
    share = right.shape[0]
    held = rows // terms
    message = 2 * held + 1

    fetch_right = pltpu.make_async_copy(right_hbm, right, sems.at[0])
    fetch_left = pltpu.make_async_copy(left_hbm, left, sems.at[1])
    fetch_psi = []
    step = blocks // 2
    for i in range(2):
        part = pl.ds(i * step, step)
        fetch_psi.append(pltpu.make_async_copy(psi_hbm.at[part], psi.at[part], sems.at[2 + i]))
    fetch_right.start()
    for fetch in fetch_psi:
        fetch.start()
    fetch_left.start()

    outbox[...] = jnp.zeros_like(outbox)
    marks[...] = jnp.zeros_like(marks)

    def clear(owner, carry):
        counts[owner] = 0
        return carry

    lax.fori_loop(0, sectors, clear, 0)

    fetch_right.wait()
    for k in range(share):
        high, low = halves(right[k])
        rights[:cols, k * cols : (k + 1) * cols] = high
        rights[cols : 2 * cols, k * cols : (k + 1) * cols] = high
        rights[2 * cols :, k * cols : (k + 1) * cols] = low

    def first(index, carry):
        value = psi[pl.ds(index * step, step)].reshape(step * rows, cols)
        high, low = halves(value)
        stacked = jnp.concatenate([high, low, high], axis=1)
        value = jnp.dot(stacked, rights[...], preferred_element_type=F32)
        high, low = halves(value)
        for b in range(step):
            for k in range(share):
                at = slice(k * rows, (k + 1) * rows)
                part = (slice(b * rows, (b + 1) * rows), slice(k * cols, (k + 1) * cols))
                middle[index * step + b, at, :cols] = high[part]
                middle[index * step + b, at, cols:] = low[part]
        return carry

    for index, fetch in enumerate(fetch_psi):
        fetch.wait()
        first(index, 0)

    fetch_left.wait()
    for r in range(rows):
        slab = jnp.concatenate([left[k, r] for k in range(share)], axis=0)
        turned[r * blocks : (r + 1) * blocks, :] = slab.T

    lane = lax.broadcasted_iota(jnp.int32, (1, cols), 1)
    for q in range(blocks):
        target = dest_ref[q]
        owner, local = target // blocks, target % blocks
        slot = counts[owner]
        counts[owner] = slot + 1
        places[q] = owner * terms * message + slot * held
        marks[pl.ds(owner, 1), :] += (lane == slot * blocks + local).astype(F32)

    outgoing = outbox.reshape(sectors + 1, terms * message, cols)
    pushes, sent = [], 0
    for begin, end, ready in ((0, 16, 32), (16, 32, 72)):
        span = end - begin
        for q in range(blocks):
            mine = turned[pl.ds(begin * blocks + q, span, stride=blocks), :]
            high, low = halves(mine)
            both = jnp.dot(
                jnp.concatenate([high, low], axis=0), middle[q], preferred_element_type=F32
            )
            item = both[:span, :cols] + (both[:span, cols:] + both[span:, :cols])
            for at in range(0, span, held):
                row = places[q] + (begin + at) // held * message
                outbox[pl.ds(row, held), :] = item[at : at + held]
        for piece in range(begin // held, end // held):
            at = piece * message + 2 * held
            outbox[pl.ds(at, sectors, stride=terms * message), :] = marks[:sectors, :]
        part = pl.ds(sent, ready - sent)
        push = pltpu.make_async_copy(
            outgoing.at[pl.ds(0, sectors), part], out_hbm.at[:, part], sems.at[len(pushes)]
        )
        push.start()
        pushes.append(push)
        sent = ready
    for push in pushes:
        push.wait()


def products(dest, psi, left_env, right_env, sectors, terms):
    blocks, rows, cols = psi.shape
    share = right_env.shape[0]
    message = 2 * (rows // terms) + 1
    total = sectors * terms * message
    hbm = pl.BlockSpec(memory_space=pltpu.HBM)
    out = pl.pallas_call(
        functools.partial(product_kernel, sectors, terms),
        in_specs=[pl.BlockSpec(memory_space=pltpu.SMEM), hbm, hbm, hbm],
        out_specs=hbm,
        out_shape=jax.ShapeDtypeStruct((sectors, terms * message, cols), F32),
        scratch_shapes=[
            pltpu.VMEM((blocks, rows, cols), F32),
            pltpu.VMEM((share, rows, rows, blocks), F32),
            pltpu.VMEM((share, cols, cols), F32),
            pltpu.VMEM((rows * blocks + blocks, share * rows), F32),
            pltpu.VMEM((3 * cols, share * cols), BF16),
            pltpu.SMEM((sectors,), jnp.int32),
            pltpu.SMEM((blocks,), jnp.int32),
            pltpu.VMEM((total + terms * message, cols), F32),
            pltpu.VMEM((sectors + 8, cols), F32),
            pltpu.VMEM((blocks, share * rows, 2 * cols), BF16),
            pltpu.SemaphoreType.DMA((4,)),
        ],
        compiler_params=pltpu.CompilerParams(vmem_limit_bytes=60 * 1024 * 1024),
    )(dest, psi, jnp.transpose(left_env, (1, 2, 3, 0)), right_env)
    return out.reshape(sectors * terms, message, 1, cols)


def combine_kernel(message, term_ref, inbox_ref, live_ref, out_ref, total):
    cols = inbox_ref.shape[-1]
    blocks, rows = out_ref.shape[0], out_ref.shape[1]
    peers = inbox_ref.shape[0] // message
    step = 128
    for index in range(peers // step):

        def row(r):
            return inbox_ref[pl.ds(index * step * message + r, step, stride=message), :]

        select = row(2 * rows).astype(BF16).T
        select = jnp.concatenate([select[:blocks], select[blocks:]], axis=1)
        for r in range(rows):
            got = jnp.concatenate([row(r), row(rows + r)], axis=0)
            high, low = halves(got)
            both = jnp.dot(select, jnp.concatenate([high, low], axis=1), preferred_element_type=F32)
            value = both[:, :cols] + both[:, cols:]
            at = slice(r * cols, (r + 1) * cols)
            total[:, at] = value if index == 0 else total[:, at] + value
    for r in range(rows):
        alive = term_ref[0] * rows + r < live_ref[...]
        out_ref[:, r, :] = jnp.where(alive, total[:, r * cols : (r + 1) * cols], 0.0)


def combine(term, inbox, block_rows, rows):
    peers, message, _, cols = inbox.shape
    blocks = block_rows.shape[0]
    vmem = pl.BlockSpec(memory_space=pltpu.VMEM)
    return pl.pallas_call(
        functools.partial(combine_kernel, message),
        in_specs=[pl.BlockSpec(memory_space=pltpu.SMEM), vmem, vmem],
        out_specs=vmem,
        out_shape=jax.ShapeDtypeStruct((blocks, rows, cols), F32),
        scratch_shapes=[pltpu.VMEM((blocks, rows * cols), F32)],
        compiler_params=pltpu.CompilerParams(vmem_limit_bytes=40 * 1024 * 1024),
    )(term, inbox.reshape(peers * message, cols), block_rows.reshape(blocks, 1))


def per_device(psi, left_env, right_env, dest, block_rows):
    sectors, terms = lax.axis_size("sector"), lax.axis_size("term")
    rows = psi.shape[1] // terms
    outbox = products(dest.reshape(-1), psi, left_env, right_env, sectors, terms)
    inbox = lax.all_to_all(outbox, ("sector", "term"), split_axis=0, concat_axis=0, tiled=True)
    term = lax.axis_index("term").reshape(1)
    return combine(term, inbox, block_rows, rows)


def solution(mesh):
    in_specs = (
        P("sector", None, None),
        P("sector", "term", None, None),
        P("term", None, None),
        P("sector", "term"),
        P("sector"),
    )
    out_specs = P("sector", "term", None)
    return jax.shard_map(
        per_device, mesh=mesh, in_specs=in_specs, out_specs=out_specs, check_vma=False
    )
```

```python
import functools

import jax
import jax.numpy as jnp
from jax import lax
from jax.experimental import pallas as pl
from jax.experimental.pallas import tpu as pltpu
from jax.sharding import PartitionSpec as P

BF16, F32 = jnp.bfloat16, jnp.float32


def halves(x):
    high = x.astype(BF16)
    return high, (x - high.astype(F32)).astype(BF16)


def product_kernel(
    sectors, terms,
    dest_ref, psi_hbm, left_hbm, right_hbm, out_hbm,
    psi, left, right, turned, rights, counts, places, outbox, marks, middle, sems,
):
    blocks, rows, cols = psi.shape
    share = right.shape[0]
    held = rows // terms
    message = 2 * held + 1

    fetch_right = pltpu.make_async_copy(right_hbm, right, sems.at[0])
    fetch_left = pltpu.make_async_copy(left_hbm, left, sems.at[1])
    fetch_psi = []
    step = blocks // 2
    for i in range(2):
        part = pl.ds(i * step, step)
        fetch_psi.append(pltpu.make_async_copy(psi_hbm.at[part], psi.at[part], sems.at[2 + i]))
    fetch_right.start()
    for fetch in fetch_psi:
        fetch.start()
    fetch_left.start()

    outbox[...] = jnp.zeros_like(outbox)
    marks[...] = jnp.zeros_like(marks)

    def clear(owner, carry):
        counts[owner] = 0
        return carry

    lax.fori_loop(0, sectors, clear, 0)

    fetch_right.wait()
    for k in range(share):
        high, low = halves(right[k])
        rights[:cols, k * cols : (k + 1) * cols] = high
        rights[cols : 2 * cols, k * cols : (k + 1) * cols] = high
        rights[2 * cols :, k * cols : (k + 1) * cols] = low

    def first(index, carry):
        value = psi[pl.ds(index * step, step)].reshape(step * rows, cols)
        high, low = halves(value)
        stacked = jnp.concatenate([high, low, high], axis=1)
        value = jnp.dot(stacked, rights[...], preferred_element_type=F32)
        high, low = halves(value)
        for b in range(step):
            for k in range(share):
                at = slice(k * rows, (k + 1) * rows)
                part = (slice(b * rows, (b + 1) * rows), slice(k * cols, (k + 1) * cols))
                middle[index * step + b, at, :cols] = high[part]
                middle[index * step + b, at, cols:] = low[part]
        return carry

    for index, fetch in enumerate(fetch_psi):
        fetch.wait()
        first(index, 0)

    fetch_left.wait()
    for r in range(rows):
        slab = jnp.concatenate([left[k, r] for k in range(share)], axis=0)
        turned[r * blocks : (r + 1) * blocks, :] = slab.T

    lane = lax.broadcasted_iota(jnp.int32, (1, cols), 1)
    for q in range(blocks):
        target = dest_ref[q]
        owner, local = target // blocks, target % blocks
        slot = counts[owner]
        counts[owner] = slot + 1
        places[q] = owner * terms * message + slot * held
        marks[pl.ds(owner, 1), :] += (lane == slot * blocks + local).astype(F32)

    for q in range(blocks):
        high, low = halves(turned[pl.ds(q, rows, stride=blocks), :])
        both = jnp.dot(
            jnp.concatenate([high, low], axis=0), middle[q], preferred_element_type=F32
        )
        item = both[:rows, :cols] + (both[:rows, cols:] + both[rows:, :cols])
        for piece in range(terms):
            at = places[q] + piece * message
            outbox[pl.ds(at, held), :] = item[piece * held : (piece + 1) * held]
    for piece in range(terms):
        at = piece * message + 2 * held
        outbox[pl.ds(at, sectors, stride=terms * message), :] = marks[:sectors, :]
    total = sectors * terms * message
    push = pltpu.make_async_copy(outbox.at[pl.ds(0, total)], out_hbm, sems.at[0])
    push.start()
    push.wait()


def products(dest, psi, left_env, right_env, sectors, terms):
    blocks, rows, cols = psi.shape
    share = right_env.shape[0]
    message = 2 * (rows // terms) + 1
    total = sectors * terms * message
    hbm = pl.BlockSpec(memory_space=pltpu.HBM)
    out = pl.pallas_call(
        functools.partial(product_kernel, sectors, terms),
        in_specs=[pl.BlockSpec(memory_space=pltpu.SMEM), hbm, hbm, hbm],
        out_specs=hbm,
        out_shape=jax.ShapeDtypeStruct((total, cols), F32),
        scratch_shapes=[
            pltpu.VMEM((blocks, rows, cols), F32),
            pltpu.VMEM((share, rows, rows, blocks), F32),
            pltpu.VMEM((share, cols, cols), F32),
            pltpu.VMEM((rows * blocks + blocks, share * rows), F32),
            pltpu.VMEM((3 * cols, share * cols), BF16),
            pltpu.SMEM((sectors,), jnp.int32),
            pltpu.SMEM((blocks,), jnp.int32),
            pltpu.VMEM((total + terms * message + 8, cols), F32),
            pltpu.VMEM((sectors + 8, cols), F32),
            pltpu.VMEM((blocks, share * rows, 2 * cols), BF16),
            pltpu.SemaphoreType.DMA((4,)),
        ],
        compiler_params=pltpu.CompilerParams(vmem_limit_bytes=60 * 1024 * 1024),
    )(dest, psi, jnp.transpose(left_env, (1, 2, 3, 0)), right_env)
    return out.reshape(sectors * terms, message, 1, cols)


def combine_kernel(message, term_ref, inbox_ref, live_ref, out_ref, total):
    cols = inbox_ref.shape[-1]
    blocks, rows = out_ref.shape[0], out_ref.shape[1]
    peers = inbox_ref.shape[0] // message
    step = 128
    for index in range(peers // step):

        def row(r):
            return inbox_ref[pl.ds(index * step * message + r, step, stride=message), :]

        select = row(2 * rows).astype(BF16).T
        select = jnp.concatenate([select[:blocks], select[blocks:]], axis=1)
        for r in range(rows):
            got = jnp.concatenate([row(r), row(rows + r)], axis=0)
            high, low = halves(got)
            both = jnp.dot(select, jnp.concatenate([high, low], axis=1), preferred_element_type=F32)
            value = both[:, :cols] + both[:, cols:]
            at = slice(r * cols, (r + 1) * cols)
            total[:, at] = value if index == 0 else total[:, at] + value
    for r in range(rows):
        alive = term_ref[0] * rows + r < live_ref[...]
        out_ref[:, r, :] = jnp.where(alive, total[:, r * cols : (r + 1) * cols], 0.0)


def combine(term, inbox, block_rows, rows):
    peers, message, _, cols = inbox.shape
    blocks = block_rows.shape[0]
    vmem = pl.BlockSpec(memory_space=pltpu.VMEM)
    return pl.pallas_call(
        functools.partial(combine_kernel, message),
        in_specs=[pl.BlockSpec(memory_space=pltpu.SMEM), vmem, vmem],
        out_specs=vmem,
        out_shape=jax.ShapeDtypeStruct((blocks, rows, cols), F32),
        scratch_shapes=[pltpu.VMEM((blocks, rows * cols), F32)],
        compiler_params=pltpu.CompilerParams(vmem_limit_bytes=60 * 1024 * 1024),
    )(term, inbox.reshape(peers * message, cols), block_rows.reshape(blocks, 1))


def per_device(psi, left_env, right_env, dest, block_rows):
    sectors, terms = lax.axis_size("sector"), lax.axis_size("term")
    rows = psi.shape[1] // terms
    outbox = products(dest.reshape(-1), psi, left_env, right_env, sectors, terms)
    inbox = lax.all_to_all(outbox, ("sector", "term"), split_axis=0, concat_axis=0, tiled=True)
    term = lax.axis_index("term").reshape(1)
    return combine(term, inbox, block_rows, rows)


def solution(mesh):
    in_specs = (
        P("sector", None, None),
        P("sector", "term", None, None),
        P("term", None, None),
        P("sector", "term"),
        P("sector"),
    )
    out_specs = P("sector", "term", None)
    return jax.shard_map(
        per_device, mesh=mesh, in_specs=in_specs, out_specs=out_specs, check_vma=False
    )
```
